256 devices in a mesh: gossip: 16 (over z_lo, x, core), fsdp: 16 (over y, z_hi).
Axes of the slice: x: 4, y: 4, z: 8 (z_hi: 4, z_lo: 2; z = z_hi * 2 + z_lo), core: 2. Of those that a mesh axis runs over, the one named last changes fastest.
Arguments:
- step_index: int32 [1], replicated, may hold values from 0 to 63
- weights: float32 [16, 4096, 1024], P('gossip', 'fsdp'), may hold values from -0.09375 to 0.09375
- momentum: float32 [16, 4096, 1024], P('gossip', 'fsdp'), may hold values from -3 to 3
- second_moment: float32 [16, 4096, 1024], P('gossip', 'fsdp'), may hold values from 0.05 to 1
- gradients: bfloat16 [2, 16, 4096, 1024], P(None, 'gossip', 'fsdp'), may hold values from -6 to 6
- tokens: bfloat16 [16, 7168, 4096], P('gossip', 'fsdp'), may hold values from -6 to 6
Outputs:
- new_weights: float32 [16, 4096, 1024], P('gossip', 'fsdp')
- new_momentum: float32 [16, 4096, 1024], P('gossip', 'fsdp')
- new_second: float32 [16, 4096, 1024], P('gossip', 'fsdp')
- projected: float32 [16, 7168, 1024], P('gossip', 'fsdp')
The draws below stay inside these ranges and needn't reach their ends.
All inputs are finite; a program needn't handle non-finite values.
Results may differ from the reference program's by a relative error of at most 0.0003.
The reference program's roundings to bfloat16 on the way count: a program that leaves them out, or rounds other values in their place, can miss the bound.
Values may be sent and summed in bfloat16 or wider, within the bound.
A program may use at most 128 MiB of HBM per device.

```python
import math
import jax
import jax.numpy as jnp
from jax import lax

D = 4096
KVW = 1024
STEPS = 2
REPLICAS = 16
TOKENS = 7168
N_GOSSIP = 16


def block_scale(key, dims, split, smallest, high):
    factor_of, own = 1.0, jax.random.fold_in(key, 6)
    for axis_at, blocks in split:
        steps = jnp.exp(jax.random.uniform(jax.random.fold_in(own, axis_at), (blocks,), jnp.float32, smallest / len(split), high / len(split)))
        factor_of = factor_of * jnp.repeat(steps, dims[axis_at] // blocks).reshape([-1 if axis == axis_at else 1 for axis in range(len(dims))])
    return factor_of


def bell_draw(own_key, shape, scale, bound, cuts=(), kind=jnp.bfloat16):
    entries = jax.random.normal(own_key, shape, jnp.float32) * scale
    if len(cuts) > 0:
        entries = block_scale(own_key, shape, cuts, -0.22, 0.18) * entries
    return jnp.clip(entries, min=-bound, max=bound).astype(kind)


def setup_inputs(seed: int = 0) -> dict:
    key_list = jax.random.split(jax.random.key(seed), 7)
    return {
        "step_index": jax.random.randint(key_list[0], (1,), 0, 64).astype(jnp.int32),
        "weights": bell_draw(key_list[1], (REPLICAS, D, KVW), D ** -0.5, 0.09375, ((0, 16), (1, 16)), jnp.float32),
        "momentum": bell_draw(key_list[2], (REPLICAS, D, KVW), 0.5, 3.0, ((0, 16), (1, 16)), jnp.float32),
        "second_moment": jnp.clip(jnp.exp(math.log(1.0) - 2.9957323 * jax.random.uniform(key_list[3], (REPLICAS, D, KVW), jnp.float32) ** block_scale(key_list[3], (REPLICAS, D, KVW), ((0, 16), (1, 16)), -0.2, 0.2)), 0.05, 1.0),
        "gradients": bell_draw(key_list[4], (STEPS, REPLICAS, D, KVW), 1.0, 6.0, ((1, 16), (2, 16))),
        "tokens": bell_draw(key_list[5], (REPLICAS, TOKENS, D), 1.0, 6.0, ((0, 16), (1, 16))),
    }


BETA_ONE = 0.9
BETA_TWO = 0.95
RATE = 0.003
DECAY = 0.1
EPSILON = 1e-08

def adam_step(avg_w, avg_m, second, grad, count):
    gradf = grad.astype(jnp.float32)
    moment = BETA_ONE * avg_m + (1.0 - BETA_ONE) * gradf
    second = BETA_TWO * second + (1.0 - BETA_TWO) * gradf * gradf
    corr_one = 1.0 - jnp.power(jnp.float32(BETA_ONE), count)
    corr_two = 1.0 - jnp.power(jnp.float32(BETA_TWO), count)
    update = moment / corr_one / (jnp.sqrt(second / corr_two) + EPSILON) + DECAY * avg_w
    return (avg_w - RATE * update, moment, second)

def reference(step_index, weights, momentum, second_moment, gradients, tokens):
    levels = N_GOSSIP.bit_length() - 1
    replica = jnp.arange(N_GOSSIP, dtype=jnp.int32)
    for step in range(STEPS):
        now = step_index[0].astype(jnp.int32) + step
        bit_now = jnp.mod(now, levels)
        partner = jnp.bitwise_xor(replica, jnp.left_shift(jnp.int32(1), bit_now))
        avg_w = 0.5 * (weights + weights[partner])
        avg_m = 0.5 * (momentum + momentum[partner])
        count = (now + 1).astype(jnp.float32)
        weights, momentum, second_moment = adam_step(avg_w, avg_m, second_moment, gradients[step], count)
    rounded = weights.astype(jnp.bfloat16)

    def forward(pair):
        return jnp.dot(pair[0], pair[1], preferred_element_type=jnp.float32)
    projected = lax.map(forward, (tokens, rounded))
    return (weights, momentum, second_moment, projected)
```

```python
from functools import partial

import jax
import jax.numpy as jnp
from jax import lax
from jax.experimental import pallas as pl
from jax.experimental.pallas import tpu as pltpu
from jax.sharding import PartitionSpec as P

BETA_ONE = 0.9
BETA_TWO = 0.95
RATE = 0.003
DECAY = 0.1
EPSILON = 1e-08

LEVELS = 4
D = 4096
KVW = 1024
ROWS = 256
TOK = 448
R = 128
H = ROWS // R
HALF = R // 2
COLS = 128
NB = KVW // COLS
NC = NB * H
AHEAD = 2
LAG_TWO, LAG_Z1, LAG_Z2, LAG_Y1, LAG_Y1F, LAG_Y2, LAG_END = 1, 2, 3, 3, 4, 4, 5
DEEP = 1024


def adam(w, m, far_w, far_m, v, g, inv_one, inv_two):
    gf = g.astype(jnp.float32)
    avg_w = 0.5 * (w + far_w)
    avg_m = 0.5 * (m + far_m)
    moment = BETA_ONE * avg_m + (1.0 - BETA_ONE) * gf
    second = BETA_TWO * v + (1.0 - BETA_TWO) * gf * gf
    update = (moment * inv_one) / (jnp.sqrt(second * inv_two) + EPSILON) + DECAY * avg_w
    return avg_w - RATE * update, moment, second


def kernel(levels, wide, corr, w, m, v, g, tok, new_w, new_m, new_v, proj,
           wm, vs, gs, toks, rx_one, tx_two, rx_two, gat,
           in_wm, in_v, in_g, in_tok, s_one, s_two, s_gat, r_one, r_two,
           r_z1, r_z2, r_y1, r_y1n, r_y1f, r_y2, r_end):
    gossip = lax.axis_index("gossip")
    me = lax.axis_index("fsdp")
    y, z = me // 4, me % 4

    def at(dy, dz):
        return ((y + dy) % 4) * 4 + (z + dz) % 4

    def partner(level):
        apart = 1 << level
        return gossip + apart * (1 - 2 * ((gossip // apart) % 2))

    first, then = partner(levels[0]), partner(levels[1])
    y_up, y_down, z_up, z_down = at(1, 0), at(3, 0), at(0, 1), at(0, 3)

    def rows_of(c):
        return pl.ds(pl.multiple_of((c % H) * R, R), R)

    def cols_of(c):
        return pl.ds(pl.multiple_of((c // H) * COLS, COLS), COLS)

    def piece(c, owner):
        return gat.at[c // H, pl.ds(pl.multiple_of(owner * ROWS + (c % H) * R, R), R), :]

    def half(c, owner, which):
        start = owner * ROWS + (c % H) * R + which * HALF
        return gat.at[c // H, pl.ds(pl.multiple_of(start, HALF), HALF), :]

    def wait_pieces(c, count, sem):
        ref = gat.at[c // H, pl.ds(0, count * R), :]
        pltpu.make_async_copy(ref, ref, sem.at[c]).wait()

    def wait_for(ref, sem):
        pltpu.make_async_copy(ref, ref, sem).wait()

    def give(ref, c, sem, to):
        pltpu.make_async_remote_copy(
            src_ref=ref, dst_ref=ref, send_sem=s_gat.at[c], recv_sem=sem.at[c],
            device_id={"fsdp": to}, device_id_type=pl.DeviceIdType.MESH).start()

    def fetch(c, _):
        pltpu.make_async_copy(w.at[0, rows_of(c), cols_of(c)], wm.at[c, 0], in_wm.at[c]).start()
        pltpu.make_async_copy(m.at[0, rows_of(c), cols_of(c)], wm.at[c, 1], in_wm.at[c]).start()
        pltpu.make_async_copy(v.at[0, rows_of(c), cols_of(c)], vs.at[c], in_v.at[c]).start()
        pltpu.make_async_copy(g.at[:, 0, rows_of(c), cols_of(c)], gs.at[c], in_g.at[c]).start()
        return 0

    lax.fori_loop(0, NC, fetch, 0)
    pltpu.make_async_copy(tok.at[0], toks, in_tok).start()

    barrier = pltpu.get_barrier_semaphore()
    for other in (first, then):
        pl.semaphore_signal(barrier, inc=1, device_id={"gossip": other}, device_id_type=pl.DeviceIdType.MESH)
    for other in (y_up, y_down, z_up, z_down):
        pl.semaphore_signal(barrier, inc=1, device_id={"fsdp": other}, device_id_type=pl.DeviceIdType.MESH)
    pl.semaphore_wait(barrier, 6)

    def send_one(c):
        wait_for(wm.at[c], in_wm.at[c])
        pltpu.make_async_remote_copy(
            src_ref=wm.at[c], dst_ref=rx_one.at[c], send_sem=s_one.at[c], recv_sem=r_one.at[c],
            device_id={"gossip": first}, device_id_type=pl.DeviceIdType.MESH).start()

    def step_one(c):
        wait_for(vs.at[c], in_v.at[c])
        wait_for(gs.at[c], in_g.at[c])
        wait_for(rx_one.at[c], r_one.at[c])
        nw, nm, nv = adam(wm[c, 0], wm[c, 1], rx_one[c, 0], rx_one[c, 1], vs[c], gs[c, 0], corr[0], corr[1])
        tx_two[c, 0] = nw
        tx_two[c, 1] = nm
        vs[c] = nv
        pltpu.make_async_remote_copy(
            src_ref=tx_two.at[c], dst_ref=rx_two.at[c], send_sem=s_two.at[c], recv_sem=r_two.at[c],
            device_id={"gossip": then}, device_id_type=pl.DeviceIdType.MESH).start()

    def step_two(c):
        wait_for(rx_two.at[c], r_two.at[c])
        nw, nm, nv = adam(tx_two[c, 0], tx_two[c, 1], rx_two[c, 0], rx_two[c, 1], vs[c], gs[c, 1], corr[2], corr[3])
        new_w[0, rows_of(c), cols_of(c)] = nw
        new_m[0, rows_of(c), cols_of(c)] = nm
        new_v[0, rows_of(c), cols_of(c)] = nv
        own = pl.ds(pl.multiple_of(me * ROWS + (c % H) * R, R), R)
        gat[c // H, own, :] = nw.astype(jnp.bfloat16)
        mine = piece(c, me)
        give(mine, c, r_z1, z_up)
        give(mine, c, r_z1, z_down)
        give(mine, c, r_y1, y_up)
        give(mine, c, r_y1, y_down)

    def z_one(c):
        wait_pieces(c, 2, r_z1)
        give(half(c, z_down, 0), c, r_z2, z_up)
        give(half(c, z_up, 1), c, r_z2, z_down)
        for owner in (z_down, z_up):
            give(piece(c, owner), c, r_y1n, y_up)
            give(piece(c, owner), c, r_y1n, y_down)

    def z_two(c):
        wait_pieces(c, 1, r_z2)
        give(piece(c, at(0, 2)), c, r_y1f, y_up)
        give(piece(c, at(0, 2)), c, r_y1f, y_down)

    def y_one(c):
        wait_pieces(c, 2, r_y1)
        give(half(c, at(3, 0), 0), c, r_y2 if wide else r_end, y_up)
        give(half(c, at(1, 0), 1), c, r_y2 if wide else r_end, y_down)
        if not wide:
            wait_pieces(c, 4, r_y1n)
            for dz in (1, 3):
                give(half(c, at(3, dz), 0), c, r_end, y_up)
                give(half(c, at(1, dz), 1), c, r_end, y_down)

    def y_one_far(c):
        wait_pieces(c, 2, r_y1f)
        give(half(c, at(3, 2), 0), c, r_end, y_up)
        give(half(c, at(1, 2), 1), c, r_end, y_down)

    def y_two(c):
        if wide:
            wait_pieces(c, 1, r_y2)
            for which in (0, 1):
                give(half(c, at(2, 0), which), c, r_end, z_up)
                give(half(c, at(2, 0), which), c, r_end, z_down)

    def finish(c):
        if wide:
            wait_pieces(c, 4, r_y1n)
            wait_pieces(c, 3, r_end)
        else:
            wait_pieces(c, 4, r_end)

        @pl.when(c % (2 * H) == 2 * H - 1)
        def _():
            pair = c // (2 * H)

            @pl.when(pair == 0)
            def _():
                wait_for(toks, in_tok)

            out = pl.ds(pl.multiple_of(pair * 2 * COLS, 2 * COLS), 2 * COLS)
            for part in range(D // DEEP):
                deep = pl.ds(part * DEEP, DEEP)
                both = jnp.concatenate([gat[2 * pair, deep, :], gat[2 * pair + 1, deep, :]], axis=1)
                add = jnp.dot(toks[:, deep], both, preferred_element_type=jnp.float32)
                if part == 0:
                    proj[0, :, out] = add
                else:
                    proj[0, :, out] += add

    def start(c, _):
        send_one(c)
        return 0

    lax.fori_loop(0, AHEAD, start, 0)

    stages = ((-AHEAD, send_one), (0, step_one), (LAG_TWO, step_two), (LAG_Z1, z_one), (LAG_Z2, z_two),
              (LAG_Y1, y_one), (LAG_Y1F, y_one_far), (LAG_Y2, y_two), (LAG_END, finish))

    def tick(t, _):
        for lag, stage in stages:
            c = t - lag

            @pl.when((c >= 0) & (c < NC))
            def _(c=c, stage=stage):
                stage(c)

        return 0

    lax.fori_loop(0, NC + LAG_END, tick, 0)

    def drain(c, _):
        wait_for(wm.at[c], s_one.at[c])
        wait_for(tx_two.at[c], s_two.at[c])
        wait_pieces(c, 15, s_gat)
        return 0

    lax.fori_loop(0, NC, drain, 0)


def fused(case, corr, w, m, v, g, tok):
    levels = (case, (case + 1) % LEVELS)
    wide = LEVELS - 1 not in levels
    dma = pltpu.SemaphoreType.DMA
    f32, bf16 = jnp.float32, jnp.bfloat16
    block = jax.ShapeDtypeStruct((1, ROWS, KVW), f32)
    hbm = pl.BlockSpec(memory_space=pl.ANY)
    vmem = pl.BlockSpec(memory_space=pltpu.VMEM)
    return pl.pallas_call(
        partial(kernel, levels, wide),
        out_shape=(block, block, block, jax.ShapeDtypeStruct((1, TOK, KVW), f32)),
        in_specs=[pl.BlockSpec(memory_space=pltpu.SMEM)] + [hbm] * 5,
        out_specs=(vmem,) * 4,
        scratch_shapes=[
            pltpu.VMEM((NC, 2, R, COLS), f32),
            pltpu.VMEM((NC, R, COLS), f32),
            pltpu.VMEM((NC, 2, R, COLS), bf16),
            pltpu.VMEM((TOK, D), bf16),
            pltpu.VMEM((NC, 2, R, COLS), f32),
            pltpu.VMEM((NC, 2, R, COLS), f32),
            pltpu.VMEM((NC, 2, R, COLS), f32),
            pltpu.VMEM((NB, D, COLS), bf16),
            dma((NC,)), dma((NC,)), dma((NC,)), dma,
        ] + [dma((NC,)) for _ in range(12)],
        compiler_params=pltpu.CompilerParams(
            collective_id=case, has_side_effects=True, vmem_limit_bytes=56 * 1024 * 1024),
        name="steps_%d" % case,
    )(corr, w, m, v, g, tok)


def per_device(step_index, weights, momentum, second_moment, gradients, tokens):
    now = step_index[0]
    counts = (now + jnp.arange(1, 3, dtype=jnp.int32)).astype(jnp.float32)
    inv_one = 1.0 / (1.0 - jnp.power(jnp.float32(BETA_ONE), counts))
    inv_two = 1.0 / (1.0 - jnp.power(jnp.float32(BETA_TWO), counts))
    corr = jnp.stack([inv_one[0], inv_two[0], inv_one[1], inv_two[1]])
    return lax.switch(
        jnp.mod(now, LEVELS), [partial(fused, case) for case in range(LEVELS)],
        corr, weights, momentum, second_moment, gradients, tokens)


def solution(mesh):
    split = P("gossip", "fsdp", None)
    return jax.shard_map(
        per_device,
        mesh=mesh,
        in_specs=(P(), split, split, split, P(None, "gossip", "fsdp", None), split),
        out_specs=(split,) * 4,
        check_vma=False,
    )
```

```python
from functools import partial

import jax
import jax.numpy as jnp
from jax import lax
from jax.experimental import pallas as pl
from jax.experimental.pallas import tpu as pltpu
from jax.sharding import PartitionSpec as P

BETA_ONE = 0.9
BETA_TWO = 0.95
RATE = 0.003
DECAY = 0.1
EPSILON = 1e-08

LEVELS = 4
D = 4096
KVW = 1024
ROWS = 256
TOK = 448
R = 128
H = ROWS // R
HALF = R // 2
PARTS = R // 8
WORDS = 8 * (1 + PARTS // 2 + PARTS // 8)
STEPS_20 = 524287.0
FINE = 268435456.0
COLS = 128
NB = KVW // COLS
NC = NB * H
PLANS = (
    (7, 2, 4, 6, 4, 10, 8, 14),
    (2, 2, 3, 4, 3, 6, 5, 15),
    (6, 1, 2, 3, 3, 7, 7, 12),
    (2, 1, 2, 3, 3, 7, 4, 11),
)
DEEP = 1024


def adam(w, m, far_w, far_m, v, g, inv_one, inv_two):
    gf = g.astype(jnp.float32)
    avg_w = 0.5 * (w + far_w)
    avg_m = 0.5 * (m + far_m)
    moment = BETA_ONE * avg_m + (1.0 - BETA_ONE) * gf
    second = BETA_TWO * v + (1.0 - BETA_TWO) * gf * gf
    update = (moment * inv_one) / (jnp.sqrt(second * inv_two) + EPSILON) + DECAY * avg_w
    return avg_w - RATE * update, moment, second


def encode(x, put):
    parts = [x[8 * i:8 * i + 8] for i in range(PARTS)]
    top = jnp.abs(parts[0])
    for part in parts[1:]:
        top = jnp.maximum(top, jnp.abs(part))
    top = (top * FINE).astype(jnp.int32) + 1
    put(0, top)
    scale = STEPS_20 / (top.astype(jnp.float32) * (1.0 / FINE))
    whole = [jnp.round(part * scale).astype(jnp.int32) for part in parts]
    for k in range(PARTS // 2):
        put(1 + k, ((whole[2 * k] << 12) & -65536) | ((whole[2 * k + 1] >> 4) & 65535))
    for k in range(PARTS // 8):
        low = whole[8 * k] & 15
        for i in range(1, 8):
            low = low | ((whole[8 * k + i] & 15) << (4 * i))
        put(1 + PARTS // 2 + k, low)


def decode(get):
    scale = (get(0).astype(jnp.float32) * (1.0 / FINE)) * (1.0 / STEPS_20)
    parts = []
    for k in range(PARTS // 2):
        word, low = get(1 + k), get(1 + PARTS // 2 + k // 4)
        shift = 8 * (k % 4)
        first = ((word >> 16) << 4) | ((low >> shift) & 15)
        other = (((word << 16) >> 16) << 4) | ((low >> (shift + 4)) & 15)
        parts += [first.astype(jnp.float32) * scale, other.astype(jnp.float32) * scale]
    return jnp.concatenate(parts, axis=0)


def powers(base, count):
    total, square = jnp.ones(count.shape, jnp.float32), base
    for bit in range(7):
        there = ((count // (1 << bit)) % 2).astype(jnp.float32)
        total = total * (1.0 + there * (square - 1.0))
        square = square * square
    return total


def kernel(levels, wide, plan, step, w, m, v, g, tok, new_w, new_m, new_v, proj,
           gs, toks, tx_one, rx_one, tx_two, rx_two, gat,
           in_sem, s_one, s_two, s_gat, r_one, r_two,
           r_z1, r_z2, r_y1, r_y1n, r_y1f, r_y2, r_end, r_end2):
    gossip = lax.axis_index("gossip")
    me = lax.axis_index("fsdp")
    y, z = me // 4, me % 4

    def at(dy, dz):
        return ((y + dy) % 4) * 4 + (z + dz) % 4

    def partner(level):
        apart = 1 << level
        return gossip + apart * (1 - 2 * ((gossip // apart) % 2))

    first, then = partner(levels[0]), partner(levels[1])
    y_up, y_down, z_up, z_down = at(1, 0), at(3, 0), at(0, 1), at(0, 3)

    def rows_of(c):
        return pl.ds(pl.multiple_of((c % H) * R, R), R)

    def cols_of(c):
        return pl.ds(pl.multiple_of((c // H) * COLS, COLS), COLS)

    def half_rows(c, which):
        return pl.ds(pl.multiple_of((c % H) * R + which * HALF, HALF), HALF)

    def piece(c, dy, dz, rows):
        there = (z + dz) % 4
        return gat.at[c // H, (y + dy) % 4, there // 2, there % 2, rows, :]

    def two_pieces(c, dy, dz, rows):
        return gat.at[c // H, (y + dy) % 4, :, (z + dz) % 2, rows, :]

    def wait_pieces(c, count, sem):
        ref = gat.at[c // H, pl.ds(0, count // 4), :, :, pl.ds(0, R), :]
        if count < 4:
            ref = gat.at[c // H, 0, 0, 0, pl.ds(0, count * R), :] if count * R <= ROWS else (
                gat.at[c // H, 0, pl.ds(0, 1), :, pl.ds(0, R), :])
        pltpu.make_async_copy(ref, ref, sem.at[c]).wait()

    def wait_for(ref, sem):
        pltpu.make_async_copy(ref, ref, sem).wait()

    def give(ref, c, sem, to):
        pltpu.make_async_remote_copy(
            src_ref=ref, dst_ref=ref, send_sem=s_gat.at[c], recv_sem=sem.at[c],
            device_id={"fsdp": to}, device_id_type=pl.DeviceIdType.MESH).start()

    barrier = pltpu.get_barrier_semaphore()
    for other in (first, then):
        pl.semaphore_signal(barrier, inc=1, device_id={"gossip": other}, device_id_type=pl.DeviceIdType.MESH)
    for other in (y_up, y_down, z_up, z_down):
        pl.semaphore_signal(barrier, inc=1, device_id={"fsdp": other}, device_id_type=pl.DeviceIdType.MESH)

    fetches = [pltpu.make_async_copy(src, dst, in_sem.at[i]) for i, (src, dst) in enumerate((
        (w, new_w), (m, new_m), (v, new_v), (g.at[:, 0], gs), (tok.at[0], toks)))]
    for fetch in fetches:
        fetch.start()

    inv_one, inv_two = [], []
    for ahead in (1, 2):
        count = jnp.full((1, COLS), step[0] + ahead, jnp.int32)
        inv_one.append(1.0 / (1.0 - powers(BETA_ONE, count)))
        inv_two.append(1.0 / (1.0 - powers(BETA_TWO, count)))

    def code(c, tx, which, ref):
        def put(k, word):
            tx[c, which, 8 * k:8 * k + 8, :] = word

        encode(ref[0, rows_of(c), cols_of(c)], put)

    def uncode(c, rx, which):
        return decode(lambda k: rx[c, which, 8 * k:8 * k + 8, :])

    def code_both(c, tx):
        code(c, tx, 0, new_w)
        code(c, tx, 1, new_m)

    def exchange(c, tx, rx, send, recv, to):
        pltpu.make_async_remote_copy(
            src_ref=tx.at[c], dst_ref=rx.at[c], send_sem=send.at[c], recv_sem=recv.at[c],
            device_id={"gossip": to}, device_id_type=pl.DeviceIdType.MESH).start()

    def send_one(c):
        code_both(c, tx_one)
        exchange(c, tx_one, rx_one, s_one, r_one, first)

    def update(c, rx, which):
        rows, cols = rows_of(c), cols_of(c)
        nw, nm, nv = adam(new_w[0, rows, cols], new_m[0, rows, cols], uncode(c, rx, 0), uncode(c, rx, 1),
                          new_v[0, rows, cols], gs[which, rows, cols], inv_one[which], inv_two[which])
        new_w[0, rows, cols] = nw
        new_m[0, rows, cols] = nm
        new_v[0, rows, cols] = nv
        return nw

    def step_one(c):
        wait_for(rx_one.at[c], r_one.at[c])
        update(c, rx_one, 0)
        code_both(c, tx_two)
        exchange(c, tx_two, rx_two, s_two, r_two, then)

    def step_two(c):
        wait_for(rx_two.at[c], r_two.at[c])
        nw = update(c, rx_two, 1)
        gat[c // H, y, z // 2, z % 2, rows_of(c), :] = nw.astype(jnp.bfloat16)
        mine = piece(c, 0, 0, rows_of(c))
        give(mine, c, r_z1, z_up)
        give(mine, c, r_z1, z_down)
        give(mine, c, r_y1, y_up)
        give(mine, c, r_y1, y_down)

    def z_one(c):
        wait_pieces(c, 2, r_z1)
        give(piece(c, 0, 3, half_rows(c, 0)), c, r_z2, z_up)
        give(piece(c, 0, 1, half_rows(c, 1)), c, r_z2, z_down)
        both = two_pieces(c, 0, 1, rows_of(c))
        give(both, c, r_y1n, y_up)
        give(both, c, r_y1n, y_down)

    def z_two(c):
        wait_pieces(c, 1, r_z2)
        far = piece(c, 0, 2, rows_of(c))
        give(far, c, r_y1f, y_up)
        give(far, c, r_y1f, y_down)

    def y_one(c):
        wait_pieces(c, 2, r_y1)
        on = r_y2 if wide else r_end
        give(piece(c, 3, 0, half_rows(c, 0)), c, on, y_up)
        give(piece(c, 1, 0, half_rows(c, 1)), c, on, y_down)
        if not wide:
            wait_pieces(c, 4, r_y1n)
            give(two_pieces(c, 3, 1, half_rows(c, 0)), c, r_end, y_up)
            give(two_pieces(c, 1, 1, half_rows(c, 1)), c, r_end, y_down)

    def y_far(c):
        wait_pieces(c, 2, r_y1f)
        last = r_end2 if wide else r_end
        give(piece(c, 3, 2, half_rows(c, 0)), c, last, y_up)
        give(piece(c, 1, 2, half_rows(c, 1)), c, last, y_down)

    def y_two(c):
        wait_pieces(c, 1, r_y2)
        over = piece(c, 2, 0, rows_of(c))
        give(over, c, r_end, z_up)
        give(over, c, r_end, z_down)

    def finish(c):
        if wide:
            wait_pieces(c, 4, r_y1n)
            wait_pieces(c, 1, r_end2)
            wait_pieces(c, 2, r_end)
        else:
            wait_pieces(c, 4, r_end)
        wait_for(tx_one.at[c], s_one.at[c])
        wait_for(tx_two.at[c], s_two.at[c])
        wait_for(gat.at[c // H, :, :, 0, pl.ds(0, 15 * R // 8), :], s_gat.at[c])

        @pl.when(c % (2 * H) == 2 * H - 1)
        def _():
            pair = c // (2 * H)

            @pl.when(pair == 0)
            def _():
                fetches[4].wait()

            out = pl.ds(pl.multiple_of(pair * 2 * COLS, 2 * COLS), 2 * COLS)
            for part in range(4):
                both = jnp.concatenate(
                    [gat[2 * pair + k, part].reshape(DEEP, COLS) for k in (0, 1)], axis=1)
                add = jnp.dot(toks[:, part * DEEP:(part + 1) * DEEP], both, preferred_element_type=jnp.float32)
                if part == 0:
                    proj[0, :, out] = add
                else:
                    proj[0, :, out] += add

    fetches[0].wait()
    fetches[1].wait()
    code_both(0, tx_one)
    pl.semaphore_wait(barrier, 6)
    exchange(0, tx_one, rx_one, s_one, r_one, first)

    def start(c, _):
        send_one(c)
        return 0

    lax.fori_loop(1, plan[0], start, 0)
    fetches[2].wait()
    fetches[3].wait()

    stages = [(-plan[0], send_one), (0, step_one)] + [
        (lag, stage) for lag, stage in zip(plan[1:], (step_two, z_one, z_two, y_one, y_far, y_two, finish))
        if wide or stage is not y_two]

    def tick(t, _):
        for lag, stage in stages:
            c = t - lag

            @pl.when((c >= 0) & (c < NC))
            def _(c=c, stage=stage):
                stage(c)

        return 0

    lax.fori_loop(0, NC + plan[7], tick, 0)


def fused(case, step, w, m, v, g, tok):
    levels = (case, (case + 1) % LEVELS)
    wide = LEVELS - 1 not in levels
    dma = pltpu.SemaphoreType.DMA
    f32, bf16 = jnp.float32, jnp.bfloat16
    block = jax.ShapeDtypeStruct((1, ROWS, KVW), f32)
    hbm = pl.BlockSpec(memory_space=pl.ANY)
    vmem = pl.BlockSpec(memory_space=pltpu.VMEM)
    return pl.pallas_call(
        partial(kernel, levels, wide, PLANS[case]),
        out_shape=(block, block, block, jax.ShapeDtypeStruct((1, TOK, KVW), f32)),
        in_specs=[pl.BlockSpec(memory_space=pltpu.SMEM)] + [hbm] * 5,
        out_specs=(vmem,) * 4,
        scratch_shapes=[
            pltpu.VMEM((2, ROWS, KVW), bf16),
            pltpu.VMEM((TOK, D), bf16),
            pltpu.VMEM((NC, 2, WORDS, COLS), jnp.int32),
            pltpu.VMEM((NC, 2, WORDS, COLS), jnp.int32),
            pltpu.VMEM((NC, 2, WORDS, COLS), jnp.int32),
            pltpu.VMEM((NC, 2, WORDS, COLS), jnp.int32),
            pltpu.VMEM((NB, 4, 2, 2, ROWS, COLS), bf16),
            dma((5,)),
        ] + [dma((NC,)) for _ in range(13)],
        compiler_params=pltpu.CompilerParams(
            collective_id=case, has_side_effects=True, vmem_limit_bytes=56 * 1024 * 1024),
        name="steps_%d" % case,
    )(step, w, m, v, g, tok)


def per_device(step_index, weights, momentum, second_moment, gradients, tokens):
    outs = lax.switch(
        jnp.mod(step_index[0], LEVELS), [partial(fused, case) for case in range(LEVELS)],
        step_index, weights, momentum, second_moment, gradients, tokens)
    return pl.pallas_call(
        put_out,
        out_shape=tuple(jax.ShapeDtypeStruct(o.shape, o.dtype) for o in outs),
        in_specs=[pl.BlockSpec(memory_space=pltpu.VMEM)] * 4,
        out_specs=(pl.BlockSpec(memory_space=pl.ANY),) * 4,
        scratch_shapes=[pltpu.SemaphoreType.DMA((4,))],
        name="put_out",
    )(*outs)


def put_out(*refs):
    sems = refs[8]
    copies = [pltpu.make_async_copy(refs[i], refs[4 + i], sems.at[i]) for i in range(4)]
    for copy in copies:
        copy.start()
    for copy in copies:
        copy.wait()


def solution(mesh):
    split = P("gossip", "fsdp", None)
    return jax.shard_map(
        per_device,
        mesh=mesh,
        in_specs=(P(), split, split, split, P(None, "gossip", "fsdp", None), split),
        out_specs=(split,) * 4,
        check_vma=False,
    )
```

```python
from functools import partial

import jax
import jax.numpy as jnp
from jax import lax
from jax.experimental import pallas as pl
from jax.experimental.pallas import tpu as pltpu
from jax.sharding import PartitionSpec as P

BETA_ONE = 0.9
BETA_TWO = 0.95
RATE = 0.003
DECAY = 0.1
EPSILON = 1e-08

LEVELS = 4
D = 4096
KVW = 1024
ROWS = 256
TOK = 448
R = 128
H = ROWS // R
HALF = R // 2
PARTS = R // 8
WORDS = 8 * (1 + PARTS // 2 + PARTS // 16)
STEPS_18 = 131071.0
FINE = 268435456.0
COLS = 128
NB = KVW // COLS
NC = NB * H
PLANS = (
    (7, 2, 4, 6, 4, 10, 8, 14),
    (2, 2, 3, 4, 3, 6, 5, 15),
    (6, 1, 2, 3, 3, 7, 7, 12),
    (2, 1, 2, 3, 3, 7, 4, 11),
)
DEEP = 1024


def adam(w, m, far_w, far_m, v, g, inv_one, inv_two):
    gf = g.astype(jnp.float32)
    avg_w = 0.5 * (w + far_w)
    avg_m = 0.5 * (m + far_m)
    moment = BETA_ONE * avg_m + (1.0 - BETA_ONE) * gf
    second = BETA_TWO * v + (1.0 - BETA_TWO) * gf * gf
    update = (moment * inv_one) / (jnp.sqrt(second * inv_two) + EPSILON) + DECAY * avg_w
    return avg_w - RATE * update, moment, second


def encode(x, put):
    parts = [x[8 * i:8 * i + 8] for i in range(PARTS)]
    top = jnp.abs(parts[0])
    for part in parts[1:]:
        top = jnp.maximum(top, jnp.abs(part))
    top = (top * FINE).astype(jnp.int32) + 1
    put(0, top)
    scale = STEPS_18 / (top.astype(jnp.float32) * (1.0 / FINE))
    whole = [jnp.round(part * scale).astype(jnp.int32) for part in parts]
    for k in range(PARTS // 2):
        put(1 + k, ((whole[2 * k] << 14) & -65536) | ((whole[2 * k + 1] >> 2) & 65535))
    for k in range(PARTS // 16):
        low = whole[16 * k] & 3
        for i in range(1, 16):
            low = low | ((whole[16 * k + i] & 3) << (2 * i))
        put(1 + PARTS // 2 + k, low)


def decode(get):
    scale = (get(0).astype(jnp.float32) * (1.0 / FINE)) * (1.0 / STEPS_18)
    parts = []
    for k in range(PARTS // 2):
        word, low = get(1 + k), get(1 + PARTS // 2 + k // 8)
        shift = 4 * (k % 8)
        first = ((word >> 16) << 2) | ((low >> shift) & 3)
        other = (((word << 16) >> 16) << 2) | ((low >> (shift + 2)) & 3)
        parts += [first.astype(jnp.float32) * scale, other.astype(jnp.float32) * scale]
    return jnp.concatenate(parts, axis=0)


def powers(base, count):
    total, square = jnp.ones(count.shape, jnp.float32), base
    for bit in range(7):
        there = ((count // (1 << bit)) % 2).astype(jnp.float32)
        total = total * (1.0 + there * (square - 1.0))
        square = square * square
    return total


def kernel(levels, wide, plan, step, w, m, v, g, tok, new_w, new_m, new_v, proj,
           gs, toks, tx_one, rx_one, tx_two, rx_two, gat,
           in_sem, s_one, s_two, s_gat, r_one, r_two,
           r_z1, r_z2, r_y1, r_y1n, r_y1f, r_y2, r_end, r_end2):
    gossip = lax.axis_index("gossip")
    me = lax.axis_index("fsdp")
    y, z = me // 4, me % 4

    def at(dy, dz):
        return ((y + dy) % 4) * 4 + (z + dz) % 4

    def partner(level):
        apart = 1 << level
        return gossip + apart * (1 - 2 * ((gossip // apart) % 2))

    first, then = partner(levels[0]), partner(levels[1])
    y_up, y_down, z_up, z_down = at(1, 0), at(3, 0), at(0, 1), at(0, 3)

    def rows_of(c):
        return pl.ds(pl.multiple_of((c % H) * R, R), R)

    def cols_of(c):
        return pl.ds(pl.multiple_of((c // H) * COLS, COLS), COLS)

    def half_rows(c, which):
        return pl.ds(pl.multiple_of((c % H) * R + which * HALF, HALF), HALF)

    def piece(c, dy, dz, rows):
        there = (z + dz) % 4
        return gat.at[c // H, (y + dy) % 4, there // 2, there % 2, rows, :]

    def two_pieces(c, dy, dz, rows):
        return gat.at[c // H, (y + dy) % 4, :, (z + dz) % 2, rows, :]

    def wait_pieces(c, count, sem):
        ref = gat.at[c // H, pl.ds(0, count // 4), :, :, pl.ds(0, R), :]
        if count < 4:
            ref = gat.at[c // H, 0, 0, 0, pl.ds(0, count * R), :] if count * R <= ROWS else (
                gat.at[c // H, 0, pl.ds(0, 1), :, pl.ds(0, R), :])
        pltpu.make_async_copy(ref, ref, sem.at[c]).wait()

    def wait_for(ref, sem):
        pltpu.make_async_copy(ref, ref, sem).wait()

    def give(ref, c, sem, to):
        pltpu.make_async_remote_copy(
            src_ref=ref, dst_ref=ref, send_sem=s_gat.at[c], recv_sem=sem.at[c],
            device_id={"fsdp": to}, device_id_type=pl.DeviceIdType.MESH).start()

    barrier = pltpu.get_barrier_semaphore()
    for other in (first, then):
        pl.semaphore_signal(barrier, inc=1, device_id={"gossip": other}, device_id_type=pl.DeviceIdType.MESH)
    for other in (y_up, y_down, z_up, z_down):
        pl.semaphore_signal(barrier, inc=1, device_id={"fsdp": other}, device_id_type=pl.DeviceIdType.MESH)

    fetches = [pltpu.make_async_copy(src, dst, in_sem.at[i]) for i, (src, dst) in enumerate((
        (w, new_w), (m, new_m), (v, new_v), (g.at[:, 0], gs), (tok.at[0], toks)))]
    for fetch in fetches:
        fetch.start()

    inv_one, inv_two = [], []
    for ahead in (1, 2):
        count = jnp.full((1, COLS), step[0] + ahead, jnp.int32)
        inv_one.append(1.0 / (1.0 - powers(BETA_ONE, count)))
        inv_two.append(1.0 / (1.0 - powers(BETA_TWO, count)))

    def code(c, tx, which, ref):
        def put(k, word):
            tx[c, which, 8 * k:8 * k + 8, :] = word

        encode(ref[0, rows_of(c), cols_of(c)], put)

    def uncode(c, rx, which):
        return decode(lambda k: rx[c, which, 8 * k:8 * k + 8, :])

    def code_both(c, tx):
        code(c, tx, 0, new_w)
        code(c, tx, 1, new_m)

    def exchange(c, tx, rx, send, recv, to):
        pltpu.make_async_remote_copy(
            src_ref=tx.at[c], dst_ref=rx.at[c], send_sem=send.at[c], recv_sem=recv.at[c],
            device_id={"gossip": to}, device_id_type=pl.DeviceIdType.MESH).start()

    def send_one(c):
        code_both(c, tx_one)
        exchange(c, tx_one, rx_one, s_one, r_one, first)

    def update(c, rx, which):
        rows, cols = rows_of(c), cols_of(c)
        nw, nm, nv = adam(new_w[0, rows, cols], new_m[0, rows, cols], uncode(c, rx, 0), uncode(c, rx, 1),
                          new_v[0, rows, cols], gs[which, rows, cols], inv_one[which], inv_two[which])
        new_w[0, rows, cols] = nw
        new_m[0, rows, cols] = nm
        new_v[0, rows, cols] = nv
        return nw

    def step_one(c):
        wait_for(rx_one.at[c], r_one.at[c])
        update(c, rx_one, 0)
        code_both(c, tx_two)
        exchange(c, tx_two, rx_two, s_two, r_two, then)

    def step_two(c):
        wait_for(rx_two.at[c], r_two.at[c])
        nw = update(c, rx_two, 1)
        gat[c // H, y, z // 2, z % 2, rows_of(c), :] = nw.astype(jnp.bfloat16)
        mine = piece(c, 0, 0, rows_of(c))
        give(mine, c, r_z1, z_up)
        give(mine, c, r_z1, z_down)
        give(mine, c, r_y1, y_up)
        give(mine, c, r_y1, y_down)

    def z_one(c):
        wait_pieces(c, 2, r_z1)
        give(piece(c, 0, 3, half_rows(c, 0)), c, r_z2, z_up)
        give(piece(c, 0, 1, half_rows(c, 1)), c, r_z2, z_down)
        both = two_pieces(c, 0, 1, rows_of(c))
        give(both, c, r_y1n, y_up)
        give(both, c, r_y1n, y_down)

    def z_two(c):
        wait_pieces(c, 1, r_z2)
        far = piece(c, 0, 2, rows_of(c))
        give(far, c, r_y1f, y_up)
        give(far, c, r_y1f, y_down)

    def y_one(c):
        wait_pieces(c, 2, r_y1)
        on = r_y2 if wide else r_end
        give(piece(c, 3, 0, half_rows(c, 0)), c, on, y_up)
        give(piece(c, 1, 0, half_rows(c, 1)), c, on, y_down)
        if not wide:
            wait_pieces(c, 4, r_y1n)
            give(two_pieces(c, 3, 1, half_rows(c, 0)), c, r_end, y_up)
            give(two_pieces(c, 1, 1, half_rows(c, 1)), c, r_end, y_down)

    def y_far(c):
        wait_pieces(c, 2, r_y1f)
        last = r_end2 if wide else r_end
        give(piece(c, 3, 2, half_rows(c, 0)), c, last, y_up)
        give(piece(c, 1, 2, half_rows(c, 1)), c, last, y_down)

    def y_two(c):
        wait_pieces(c, 1, r_y2)
        over = piece(c, 2, 0, rows_of(c))
        give(over, c, r_end, z_up)
        give(over, c, r_end, z_down)

    def finish(c):
        if wide:
            wait_pieces(c, 4, r_y1n)
            wait_pieces(c, 1, r_end2)
            wait_pieces(c, 2, r_end)
        else:
            wait_pieces(c, 4, r_end)
        wait_for(tx_one.at[c], s_one.at[c])
        wait_for(tx_two.at[c], s_two.at[c])
        wait_for(gat.at[c // H, :, :, 0, pl.ds(0, 15 * R // 8), :], s_gat.at[c])

        @pl.when(c % (2 * H) == 2 * H - 1)
        def _():
            pair = c // (2 * H)

            @pl.when(pair == 0)
            def _():
                fetches[4].wait()

            out = pl.ds(pl.multiple_of(pair * 2 * COLS, 2 * COLS), 2 * COLS)
            for part in range(4):
                both = jnp.concatenate(
                    [gat[2 * pair + k, part].reshape(DEEP, COLS) for k in (0, 1)], axis=1)
                add = jnp.dot(toks[:, part * DEEP:(part + 1) * DEEP], both, preferred_element_type=jnp.float32)
                if part == 0:
                    proj[0, :, out] = add
                else:
                    proj[0, :, out] += add

    fetches[0].wait()
    fetches[1].wait()
    code_both(0, tx_one)
    pl.semaphore_wait(barrier, 6)
    exchange(0, tx_one, rx_one, s_one, r_one, first)

    def start(c, _):
        send_one(c)
        return 0

    lax.fori_loop(1, plan[0], start, 0)
    fetches[2].wait()
    fetches[3].wait()

    stages = [(-plan[0], send_one), (0, step_one)] + [
        (lag, stage) for lag, stage in zip(plan[1:], (step_two, z_one, z_two, y_one, y_far, y_two, finish))
        if wide or stage is not y_two]

    def tick(t, _):
        for lag, stage in stages:
            c = t - lag

            @pl.when((c >= 0) & (c < NC))
            def _(c=c, stage=stage):
                stage(c)

        return 0

    lax.fori_loop(0, NC + plan[7], tick, 0)


def fused(case, step, w, m, v, g, tok):
    levels = (case, (case + 1) % LEVELS)
    wide = LEVELS - 1 not in levels
    dma = pltpu.SemaphoreType.DMA
    f32, bf16 = jnp.float32, jnp.bfloat16
    block = jax.ShapeDtypeStruct((1, ROWS, KVW), f32)
    hbm = pl.BlockSpec(memory_space=pl.ANY)
    vmem = pl.BlockSpec(memory_space=pltpu.VMEM)
    return pl.pallas_call(
        partial(kernel, levels, wide, PLANS[case]),
        out_shape=(block, block, block, jax.ShapeDtypeStruct((1, TOK, KVW), f32)),
        in_specs=[pl.BlockSpec(memory_space=pltpu.SMEM)] + [hbm] * 5,
        out_specs=(vmem,) * 4,
        scratch_shapes=[
            pltpu.VMEM((2, ROWS, KVW), bf16),
            pltpu.VMEM((TOK, D), bf16),
            pltpu.VMEM((NC, 2, WORDS, COLS), jnp.int32),
            pltpu.VMEM((NC, 2, WORDS, COLS), jnp.int32),
            pltpu.VMEM((NC, 2, WORDS, COLS), jnp.int32),
            pltpu.VMEM((NC, 2, WORDS, COLS), jnp.int32),
            pltpu.VMEM((NB, 4, 2, 2, ROWS, COLS), bf16),
            dma((5,)),
        ] + [dma((NC,)) for _ in range(13)],
        compiler_params=pltpu.CompilerParams(
            collective_id=case, has_side_effects=True, vmem_limit_bytes=40 * 1024 * 1024),
        name="steps_%d" % case,
    )(step, w, m, v, g, tok)


def per_device(step_index, weights, momentum, second_moment, gradients, tokens):
    outs = lax.switch(
        jnp.mod(step_index[0], LEVELS), [partial(fused, case) for case in range(LEVELS)],
        step_index, weights, momentum, second_moment, gradients, tokens)
    return pl.pallas_call(
        put_out,
        out_shape=tuple(jax.ShapeDtypeStruct(o.shape, o.dtype) for o in outs),
        in_specs=[pl.BlockSpec(memory_space=pltpu.VMEM)] * 4,
        out_specs=(pl.BlockSpec(memory_space=pl.ANY),) * 4,
        scratch_shapes=[pltpu.SemaphoreType.DMA((4,))],
        compiler_params=pltpu.CompilerParams(vmem_limit_bytes=8 * 1024 * 1024),
        name="put_out",
    )(*outs)


def put_out(*refs):
    sems = refs[8]
    copies = [pltpu.make_async_copy(refs[i], refs[4 + i], sems.at[i]) for i in range(4)]
    for copy in copies:
        copy.start()
    for copy in copies:
        copy.wait()


def solution(mesh):
    split = P("gossip", "fsdp", None)
    return jax.shard_map(
        per_device,
        mesh=mesh,
        in_specs=(P(), split, split, split, P(None, "gossip", "fsdp", None), split),
        out_specs=(split,) * 4,
        check_vma=False,
    )
```

```python
from functools import partial

import jax
import jax.numpy as jnp
from jax import lax
from jax.experimental import pallas as pl
from jax.experimental.pallas import tpu as pltpu
from jax.sharding import PartitionSpec as P

BETA_ONE = 0.9
BETA_TWO = 0.95
RATE = 0.003
DECAY = 0.1
EPSILON = 1e-08

LEVELS = 4
D = 4096
KVW = 1024
ROWS = 256
TOK = 448
R = 128
H = ROWS // R
HALF = R // 2
PARTS = R // 8
WORDS = 8 * (1 + PARTS // 2 + PARTS // 16)
STEPS_18 = 131071.0
FINE = 268435456.0
COLS = 128
NB = KVW // COLS
NC = NB * H
PLANS = (
    (7, 2, 4, 6, 4, 10, 8, 14),
    (2, 2, 3, 4, 3, 6, 5, 15),
    (3, 2, 4, 6, 3, 10, 7, 14),
    (3, 1, 3, 5, 2, 9, 6, 13),
)
DEEP = 1024


def adam(w, m, far_w, far_m, v, g, inv_one, inv_two):
    gf = g.astype(jnp.float32)
    avg_w = 0.5 * (w + far_w)
    avg_m = 0.5 * (m + far_m)
    moment = BETA_ONE * avg_m + (1.0 - BETA_ONE) * gf
    second = BETA_TWO * v + (1.0 - BETA_TWO) * gf * gf
    update = (moment * inv_one) / (jnp.sqrt(second * inv_two) + EPSILON) + DECAY * avg_w
    return avg_w - RATE * update, moment, second


def encode(x, put):
    parts = [x[8 * i:8 * i + 8] for i in range(PARTS)]
    top = jnp.abs(parts[0])
    for part in parts[1:]:
        top = jnp.maximum(top, jnp.abs(part))
    top = (top * FINE).astype(jnp.int32) + 1
    put(0, top)
    scale = STEPS_18 / (top.astype(jnp.float32) * (1.0 / FINE))
    whole = [jnp.round(part * scale).astype(jnp.int32) for part in parts]
    for k in range(PARTS // 2):
        put(1 + k, ((whole[2 * k] << 14) & -65536) | ((whole[2 * k + 1] >> 2) & 65535))
    for k in range(PARTS // 16):
        low = whole[16 * k] & 3
        for i in range(1, 16):
            low = low | ((whole[16 * k + i] & 3) << (2 * i))
        put(1 + PARTS // 2 + k, low)


def decode(get):
    scale = (get(0).astype(jnp.float32) * (1.0 / FINE)) * (1.0 / STEPS_18)
    parts = []
    for k in range(PARTS // 2):
        word, low = get(1 + k), get(1 + PARTS // 2 + k // 8)
        shift = 4 * (k % 8)
        first = ((word >> 16) << 2) | ((low >> shift) & 3)
        other = (((word << 16) >> 16) << 2) | ((low >> (shift + 2)) & 3)
        parts += [first.astype(jnp.float32) * scale, other.astype(jnp.float32) * scale]
    return jnp.concatenate(parts, axis=0)


def powers(base, count):
    total, square = jnp.ones(count.shape, jnp.float32), base
    for bit in range(7):
        there = ((count // (1 << bit)) % 2).astype(jnp.float32)
        total = total * (1.0 + there * (square - 1.0))
        square = square * square
    return total


def kernel(levels, wide, plan, step, w, m, v, g, tok, new_w, new_m, new_v, proj,
           gs, toks, tx_one, rx_one, tx_two, rx_two, gat,
           in_sem, s_one, s_two, s_gat, r_one, r_two,
           r_z1, r_z2, r_y1, r_y1n, r_y1f, r_y2, r_end, r_end2):
    gossip = lax.axis_index("gossip")
    me = lax.axis_index("fsdp")
    y, z = me // 4, me % 4

    def at(dy, dz):
        return ((y + dy) % 4) * 4 + (z + dz) % 4

    def partner(level):
        apart = 1 << level
        return gossip + apart * (1 - 2 * ((gossip // apart) % 2))

    first, then = partner(levels[0]), partner(levels[1])
    y_up, y_down, z_up, z_down = at(1, 0), at(3, 0), at(0, 1), at(0, 3)

    def rows_of(c):
        return pl.ds(pl.multiple_of((c % H) * R, R), R)

    def cols_of(c):
        return pl.ds(pl.multiple_of((c // H) * COLS, COLS), COLS)

    def half_rows(c, which):
        return pl.ds(pl.multiple_of((c % H) * R + which * HALF, HALF), HALF)

    def piece(c, dy, dz, rows):
        there = (z + dz) % 4
        return gat.at[c // H, (y + dy) % 4, there // 2, there % 2, rows, :]

    def two_pieces(c, dy, dz, rows):
        return gat.at[c // H, (y + dy) % 4, :, (z + dz) % 2, rows, :]

    def wait_pieces(c, count, sem):
        ref = gat.at[c // H, pl.ds(0, count // 4), :, :, pl.ds(0, R), :]
        if count < 4:
            ref = gat.at[c // H, 0, 0, 0, pl.ds(0, count * R), :] if count * R <= ROWS else (
                gat.at[c // H, 0, pl.ds(0, 1), :, pl.ds(0, R), :])
        pltpu.make_async_copy(ref, ref, sem.at[c]).wait()

    def wait_for(ref, sem):
        pltpu.make_async_copy(ref, ref, sem).wait()

    def give(ref, c, sem, to):
        pltpu.make_async_remote_copy(
            src_ref=ref, dst_ref=ref, send_sem=s_gat.at[c], recv_sem=sem.at[c],
            device_id={"fsdp": to}, device_id_type=pl.DeviceIdType.MESH).start()

    barrier = pltpu.get_barrier_semaphore()
    for other in (first, then):
        pl.semaphore_signal(barrier, inc=1, device_id={"gossip": other}, device_id_type=pl.DeviceIdType.MESH)
    for other in (y_up, y_down, z_up, z_down):
        pl.semaphore_signal(barrier, inc=1, device_id={"fsdp": other}, device_id_type=pl.DeviceIdType.MESH)

    fetches = [pltpu.make_async_copy(src, dst, in_sem.at[i]) for i, (src, dst) in enumerate((
        (w, new_w), (m, new_m), (v, new_v), (g.at[:, 0], gs), (tok.at[0], toks)))]
    for fetch in fetches:
        fetch.start()

    inv_one, inv_two = [], []
    for ahead in (1, 2):
        count = jnp.full((1, COLS), step[0] + ahead, jnp.int32)
        inv_one.append(1.0 / (1.0 - powers(BETA_ONE, count)))
        inv_two.append(1.0 / (1.0 - powers(BETA_TWO, count)))

    def code(c, tx, which, ref):
        def put(k, word):
            tx[c, which, 8 * k:8 * k + 8, :] = word

        encode(ref[0, rows_of(c), cols_of(c)], put)

    def uncode(c, rx, which):
        return decode(lambda k: rx[c, which, 8 * k:8 * k + 8, :])

    def code_both(c, tx):
        code(c, tx, 0, new_w)
        code(c, tx, 1, new_m)

    def exchange(c, tx, rx, send, recv, to):
        pltpu.make_async_remote_copy(
            src_ref=tx.at[c], dst_ref=rx.at[c], send_sem=send.at[c], recv_sem=recv.at[c],
            device_id={"gossip": to}, device_id_type=pl.DeviceIdType.MESH).start()

    def send_one(c):
        code_both(c, tx_one)
        exchange(c, tx_one, rx_one, s_one, r_one, first)

    def update(c, rx, which):
        rows, cols = rows_of(c), cols_of(c)
        nw, nm, nv = adam(new_w[0, rows, cols], new_m[0, rows, cols], uncode(c, rx, 0), uncode(c, rx, 1),
                          new_v[0, rows, cols], gs[which, rows, cols], inv_one[which], inv_two[which])
        new_w[0, rows, cols] = nw
        new_m[0, rows, cols] = nm
        new_v[0, rows, cols] = nv
        return nw

    def step_one(c):
        wait_for(rx_one.at[c], r_one.at[c])
        update(c, rx_one, 0)
        code_both(c, tx_two)
        exchange(c, tx_two, rx_two, s_two, r_two, then)

    def step_two(c):
        wait_for(rx_two.at[c], r_two.at[c])
        nw = update(c, rx_two, 1)
        gat[c // H, y, z // 2, z % 2, rows_of(c), :] = nw.astype(jnp.bfloat16)
        mine = piece(c, 0, 0, rows_of(c))
        give(mine, c, r_z1, z_up)
        give(mine, c, r_z1, z_down)
        give(mine, c, r_y1, y_up)
        give(mine, c, r_y1, y_down)

    def z_one(c):
        wait_pieces(c, 2, r_z1)
        give(piece(c, 0, 3, half_rows(c, 0)), c, r_z2, z_up)
        give(piece(c, 0, 1, half_rows(c, 1)), c, r_z2, z_down)
        both = two_pieces(c, 0, 1, rows_of(c))
        give(both, c, r_y1n, y_up)
        give(both, c, r_y1n, y_down)

    def z_two(c):
        wait_pieces(c, 1, r_z2)
        far = piece(c, 0, 2, rows_of(c))
        give(far, c, r_y1f, y_up)
        give(far, c, r_y1f, y_down)

    def y_one(c):
        wait_pieces(c, 2, r_y1)
        on = r_y2 if wide else r_end
        give(piece(c, 3, 0, half_rows(c, 0)), c, on, y_up)
        give(piece(c, 1, 0, half_rows(c, 1)), c, on, y_down)

    def y_near(c):
        wait_pieces(c, 4, r_y1n)
        give(two_pieces(c, 3, 1, half_rows(c, 0)), c, r_end, y_up)
        give(two_pieces(c, 1, 1, half_rows(c, 1)), c, r_end, y_down)

    def y_far(c):
        wait_pieces(c, 2, r_y1f)
        last = r_end2 if wide else r_end
        give(piece(c, 3, 2, half_rows(c, 0)), c, last, y_up)
        give(piece(c, 1, 2, half_rows(c, 1)), c, last, y_down)

    def y_two(c):
        wait_pieces(c, 1, r_y2)
        over = piece(c, 2, 0, rows_of(c))
        give(over, c, r_end, z_up)
        give(over, c, r_end, z_down)

    def finish(c):
        if wide:
            wait_pieces(c, 4, r_y1n)
            wait_pieces(c, 1, r_end2)
            wait_pieces(c, 2, r_end)
        else:
            wait_pieces(c, 4, r_end)
        wait_for(tx_one.at[c], s_one.at[c])
        wait_for(tx_two.at[c], s_two.at[c])
        wait_for(gat.at[c // H, :, :, 0, pl.ds(0, 15 * R // 8), :], s_gat.at[c])

        @pl.when(c % (2 * H) == 2 * H - 1)
        def _():
            pair = c // (2 * H)

            @pl.when(pair == 0)
            def _():
                fetches[4].wait()

            out = pl.ds(pl.multiple_of(pair * 2 * COLS, 2 * COLS), 2 * COLS)
            for part in range(4):
                both = jnp.concatenate(
                    [gat[2 * pair + k, part].reshape(DEEP, COLS) for k in (0, 1)], axis=1)
                add = jnp.dot(toks[:, part * DEEP:(part + 1) * DEEP], both, preferred_element_type=jnp.float32)
                if part == 0:
                    proj[0, :, out] = add
                else:
                    proj[0, :, out] += add

    fetches[0].wait()
    fetches[1].wait()
    code_both(0, tx_one)
    pl.semaphore_wait(barrier, 6)
    exchange(0, tx_one, rx_one, s_one, r_one, first)

    def start(c, _):
        send_one(c)
        return 0

    lax.fori_loop(1, plan[0], start, 0)
    fetches[2].wait()
    fetches[3].wait()

    seventh = y_two if wide else y_near
    stages = [(-plan[0], send_one), (0, step_one)] + list(
        zip(plan[1:], (step_two, z_one, z_two, y_one, y_far, seventh, finish)))

    def tick(t, _):
        for lag, stage in stages:
            c = t - lag

            @pl.when((c >= 0) & (c < NC))
            def _(c=c, stage=stage):
                stage(c)

        return 0

    lax.fori_loop(0, NC + plan[7], tick, 0)


def fused(case, step, w, m, v, g, tok):
    levels = (case, (case + 1) % LEVELS)
    wide = LEVELS - 1 not in levels
    dma = pltpu.SemaphoreType.DMA
    f32, bf16 = jnp.float32, jnp.bfloat16
    block = jax.ShapeDtypeStruct((1, ROWS, KVW), f32)
    hbm = pl.BlockSpec(memory_space=pl.ANY)
    vmem = pl.BlockSpec(memory_space=pltpu.VMEM)
    return pl.pallas_call(
        partial(kernel, levels, wide, PLANS[case]),
        out_shape=(block, block, block, jax.ShapeDtypeStruct((1, TOK, KVW), f32)),
        in_specs=[pl.BlockSpec(memory_space=pltpu.SMEM)] + [hbm] * 5,
        out_specs=(vmem,) * 4,
        scratch_shapes=[
            pltpu.VMEM((2, ROWS, KVW), bf16),
            pltpu.VMEM((TOK, D), bf16),
            pltpu.VMEM((NC, 2, WORDS, COLS), jnp.int32),
            pltpu.VMEM((NC, 2, WORDS, COLS), jnp.int32),
            pltpu.VMEM((NC, 2, WORDS, COLS), jnp.int32),
            pltpu.VMEM((NC, 2, WORDS, COLS), jnp.int32),
            pltpu.VMEM((NB, 4, 2, 2, ROWS, COLS), bf16),
            dma((5,)),
        ] + [dma((NC,)) for _ in range(13)],
        compiler_params=pltpu.CompilerParams(
            collective_id=case, has_side_effects=True, vmem_limit_bytes=40 * 1024 * 1024),
        name="steps_%d" % case,
    )(step, w, m, v, g, tok)


def per_device(step_index, weights, momentum, second_moment, gradients, tokens):
    outs = lax.switch(
        jnp.mod(step_index[0], LEVELS), [partial(fused, case) for case in range(LEVELS)],
        step_index, weights, momentum, second_moment, gradients, tokens)
    return pl.pallas_call(
        put_out,
        out_shape=tuple(jax.ShapeDtypeStruct(o.shape, o.dtype) for o in outs),
        in_specs=[pl.BlockSpec(memory_space=pltpu.VMEM)] * 4,
        out_specs=(pl.BlockSpec(memory_space=pl.ANY),) * 4,
        scratch_shapes=[pltpu.SemaphoreType.DMA((4,))],
        compiler_params=pltpu.CompilerParams(vmem_limit_bytes=8 * 1024 * 1024),
        name="put_out",
    )(*outs)


def put_out(*refs):
    sems = refs[8]
    copies = [pltpu.make_async_copy(refs[i], refs[4 + i], sems.at[i]) for i in range(4)]
    for copy in copies:
        copy.start()
    for copy in copies:
        copy.wait()


def solution(mesh):
    split = P("gossip", "fsdp", None)
    return jax.shard_map(
        per_device,
        mesh=mesh,
        in_specs=(P(), split, split, split, P(None, "gossip", "fsdp", None), split),
        out_specs=(split,) * 4,
        check_vma=False,
    )
```
